32 devices in a mesh: groups: 2 (over x), pos: 16 (over z, y, core).
Axes of the slice: x: 2, y: 2, z: 4, core: 2. Of those that a mesh axis runs over, the one named last changes fastest.
Arguments:
- activations: bfloat16 [32768, 512], P(('groups', 'pos')), parts along dimension 0, may hold values from -6 to 6
- kernel: bfloat16 [512, 5, 608], P('pos'), may hold values from -0.125 to 0.125
- cotangent: bfloat16 [16384, 608], P(('groups', 'pos')), parts along dimension 0, may hold values from -6 to 6
Outputs:
- pooled: bfloat16 [16384, 608], P(('groups', 'pos')), parts along dimension 0
- input_grad: bfloat16 [32768, 512], P(('groups', 'pos')), parts along dimension 0
- kernel_grad: float32 [1024, 5, 608], P(('groups', 'pos')), parts along dimension 0
The draws below stay inside these ranges and needn't reach their ends.
There are 2 independent parts, one for each index of `groups`. The reference program is written for one: setup_inputs(seed, part) draws one part's arguments, and reference() takes and returns one part's arrays. A program takes and returns all parts, laid end to end along the dimension named above; an argument that names none is the same for every part. Nothing has to cross between parts.
All inputs are finite; a program needn't handle non-finite values.
Results may differ from the reference program's by a relative error of at most 0.0041.
Values may be sent and summed in bfloat16 or wider, within the bound.
No kernel may reach another device: no remote copies, remote signals or barrier semaphores. Data moves between devices by JAX's collectives and lax.ppermute only.
A program may use at most 128 MiB of HBM per device.

```python
import jax
import jax.numpy as jnp

CIN = 512
COUT = 608
KERNEL_TAPS = 5
DILATION_STEP = 4
TOKENS = 16384


def strengthened(drawn, own_key, source, target, parts, factor):
    def block_of(position):
        return (jnp.arange(drawn.shape[position]) // (drawn.shape[position] // parts)).reshape((-1,) + (1,) * (drawn.ndim - 1 - position))

    first = jax.random.permutation(own_key, parts)[block_of(target)]
    other_side = (block_of(target) + parts // 2) % parts
    return jnp.where((block_of(source) == first) | (block_of(source) == other_side), factor * drawn, drawn)


def steps_of(own_key, dims, pieces, smallest, high):
    def one(axis_at, blocks):
        steps = jax.random.uniform(jax.random.fold_in(jax.random.fold_in(own_key, 6), axis_at), (blocks,), jnp.float32, smallest / len(pieces), high / len(pieces))
        return jnp.repeat(jnp.exp(steps), dims[axis_at] // blocks).reshape((-1,) + (1,) * (len(dims) - axis_at - 1))

    loudness = one(*pieces[0])
    for cut in pieces[1:]:
        loudness = loudness * one(*cut)
    return loudness


def centred(stream_key, shape, deviation, reach, pieces=(), held_as=jnp.bfloat16):
    loudness = steps_of(stream_key, shape, pieces, -0.22, 0.18) if pieces else 1.0
    entries = jax.random.normal(stream_key, shape, jnp.float32) * deviation * loudness
    return jnp.minimum(jnp.maximum(entries, -reach), reach).astype(held_as)


def bell_draw_with(rng, extent, width, limit, shards, heavy, held_as=jnp.bfloat16):
    entries = width * jax.random.normal(rng, extent, jnp.float32)
    if shards:
        entries = entries * steps_of(rng, extent, shards, -0.22, 0.18)
    return jnp.clip(strengthened(entries, jax.random.fold_in(rng, 3), *heavy), -limit, limit).astype(held_as)


def setup_inputs(seed: int = 0, part: int = 0) -> dict:
    key_of = jax.random.split(jax.random.key(seed), 4)
    part_keys = jax.random.split(jax.random.fold_in(key_of[3], part), 4)
    return {
        "activations": bell_draw_with(part_keys[0], (TOKENS, CIN), 1.0, 6.0, ((0, 16),), (0, 1, 16, 2.0)),
        "kernel": centred(key_of[1], (CIN, KERNEL_TAPS, COUT), (CIN * KERNEL_TAPS) ** -0.5, 0.125, ((0, 16),)),
        "cotangent": centred(part_keys[2], (TOKENS // 2, COUT), 1.0, 6.0, ((0, 16),)),
    }


def gelu_value(v):
    return 0.5 * v * (1.0 + jax.scipy.special.erf(v * 0.7071067811865476))


def gelu_slope(v):
    return 0.5 * (1.0 + jax.scipy.special.erf(v * 0.7071067811865476)) + v * jnp.exp(-0.5 * v * v) * 0.3989422804014327


def reference(activations, kernel, cotangent):
    window_length = activations.shape[0]
    reach_row_count = (KERNEL_TAPS - 1) // 2 * DILATION_STEP
    values = activations.astype(jnp.float32)
    gelu = gelu_value(values).astype(jnp.bfloat16)
    padded_activation = jnp.pad(gelu, ((reach_row_count, reach_row_count), (0, 0)))
    dilated_output = jnp.zeros((window_length, kernel.shape[2]), jnp.float32)
    for tap_offset in range(KERNEL_TAPS):
        dilated_output = dilated_output + jnp.dot(padded_activation[tap_offset * DILATION_STEP:tap_offset * DILATION_STEP + window_length], kernel[:, tap_offset, :], preferred_element_type=jnp.float32)
    pooled = (0.5 * dilated_output.reshape(window_length // 2, 2, -1).sum(axis=1)).astype(jnp.bfloat16)
    convolution_gradient = (0.5 * jnp.repeat(cotangent.astype(jnp.float32), 2, axis=0)).astype(jnp.bfloat16)
    gradient_pieces = []
    for tap_offset in range(KERNEL_TAPS):
        gradient_pieces.append(jnp.dot(padded_activation[tap_offset * DILATION_STEP:tap_offset * DILATION_STEP + window_length].T, convolution_gradient, preferred_element_type=jnp.float32))
    kernel_grad = jnp.stack(gradient_pieces, axis=1)
    padded_gradient = jnp.pad(convolution_gradient, ((reach_row_count, reach_row_count), (0, 0)))
    gelu_grad = jnp.zeros((window_length, kernel.shape[0]), jnp.float32)
    for tap_offset in range(KERNEL_TAPS):
        leading_rows = (KERNEL_TAPS - 1 - tap_offset) * DILATION_STEP
        gelu_grad = gelu_grad + jnp.dot(padded_gradient[leading_rows:leading_rows + window_length], kernel[:, tap_offset, :].T, preferred_element_type=jnp.float32)
    input_grad = (gelu_grad * gelu_slope(values)).astype(jnp.bfloat16)
    return pooled, input_grad, kernel_grad
```

```python
import functools

import jax
import jax.numpy as jnp
from jax import lax
from jax.experimental import pallas as pl
from jax.experimental.pallas import tpu as pltpu
from jax.sharding import PartitionSpec as P

STEP = 4
TAPS = 5
HALO = 16
TEAM = 4
EXT = 8
VMEM = pl.BlockSpec(memory_space=pltpu.VMEM)
SMEM = pl.BlockSpec(memory_space=pltpu.SMEM)
F32 = jnp.float32
BF16 = jnp.bfloat16


def params(mib):
    return pltpu.CompilerParams(vmem_limit_bytes=mib * 2**20)


def gelu_value(v):
    return 0.5 * v * (1.0 + lax.erf(v * 0.7071067811865476))


def gelu_slope(v):
    return (
        0.5 * (1.0 + lax.erf(v * 0.7071067811865476))
        + v * jnp.exp(-0.5 * v * v) * 0.3989422804014327
    )


def relative_order(place, rows, channels, transposed):
    shape = (channels, channels)
    chan = lax.broadcasted_iota(jnp.int32, shape, 1 if transposed else 0)
    col = lax.broadcasted_iota(jnp.int32, shape, 0 if transposed else 1)
    quarter = channels // TEAM
    mate = lax.div(col, quarter)
    within = lax.rem(col, quarter)
    level = lax.div(within, rows)
    row = lax.rem(within, rows)
    want = rows * (TEAM * (level ^ place[0]) + (mate ^ place[1])) + row
    return jnp.where(chan == want, 1.0, 0.0).astype(BF16)


def pool_kernel(rows, place, act, low, high, own, near, far):
    channels = act.shape[1]
    quarter = channels // TEAM
    order = relative_order(place, rows, channels, False)

    def pooled(g):
        t = g.shape[0]
        u = lax.broadcasted_iota(jnp.int32, (t // 2, t), 0)
        v = lax.broadcasted_iota(jnp.int32, (t // 2, t), 1)
        halves = jnp.where(lax.div(v, 2) == u, 0.5, 0.0).astype(BF16)
        s = jnp.dot(halves, g, preferred_element_type=F32).astype(BF16)
        return jnp.dot(s, order, preferred_element_type=F32).astype(BF16)

    def put(at, s):
        n = s.shape[0]
        own[at : at + n, :] = s[:, :quarter]
        near[at : at + n, :] = s[:, quarter : 2 * quarter]
        far[at : at + n, :] = s[:, 2 * quarter :]

    def gelu(v):
        return gelu_value(v.astype(F32)).astype(BF16)

    window = act.shape[0]
    block = 256
    g_prev = gelu(low[...])
    for at in range(0, window, block):
        g = gelu(act[at : at + block, :])
        joined = jnp.concatenate([g_prev, g[: block - HALO]], axis=0)
        put(at // 2, pooled(joined))
        g_prev = g[block - HALO :]
    put(window // 2, pooled(jnp.concatenate([g_prev, gelu(high[...])], axis=0)))


def wgrad_kernel(rows, s0, s1, s2, s3, c0, c1, c2, c3, *refs):
    *outs, left = refs
    positions = c0.shape[1]
    quarter = s0.shape[1]
    total = None
    for s, c in ((s0, c0), (s1, c1), (s2, c2), (s3, c3)):
        for k in range(TAPS):
            at = EXT + 2 * (k - 2)
            left[k * quarter : (k + 1) * quarter, :] = s[at : at + positions, :].T
        term = lax.dot_general(
            left[...], c[...], (((1,), (1,)), ((), ())), preferred_element_type=F32
        )
        total = term if total is None else total + term
    if len(outs) == 1:
        for k in range(TAPS):
            outs[0][k] = total[k * quarter : (k + 1) * quarter]
    else:
        for k in range(TAPS):
            for m, out in enumerate(outs):
                at = k * quarter + m * rows
                out[k] = total[at : at + rows].astype(out.dtype)


def fill_ext(ext, cot, low, high):
    positions = cot.shape[0]
    ext[:HALO, :] = low[...]
    ext[HALO : HALO + positions, :] = cot[...]
    ext[HALO + positions :, :] = high[...]


def pair_products(s_pair, k_pair, ext, positions):
    acc = None
    grad = None
    for k in range(TAPS):
        at = EXT + 2 * (k - 2)
        weights = k_pair(k)
        term = jnp.dot(s_pair(at), weights, preferred_element_type=F32)
        acc = term if acc is None else acc + term
        back = HALO - 2 * (k - 2)
        term = lax.dot_general(
            ext[back : back + positions, :],
            weights,
            (((1,), (1,)), ((), ())),
            preferred_element_type=F32,
        )
        grad = term if grad is None else grad + term
    return acc, grad


def first_kernel(rows, place, own, near, k0, k1, cot, low, high, act, acc, grad, slope, ext):
    positions = cot.shape[0]
    fill_ext(ext, cot, low, high)
    acc[...], grad[...] = pair_products(
        lambda at: jnp.concatenate([own[at : at + positions], near[at : at + positions]], axis=1),
        lambda k: jnp.concatenate([k0[k], k1[k]], axis=0),
        ext,
        positions,
    )
    order = relative_order(place, rows, act.shape[1], False)
    block = 256
    for at in range(0, act.shape[0], block):
        v = jnp.dot(act[at : at + block, :], order, preferred_element_type=F32)
        slope[at : at + block, :] = 0.5 * gelu_slope(v)


def second_kernel(
    rows, place, far, k2, k3, cot, low, high, acc1, grad1, slope, pooled, out, ext, doubled
):
    positions = cot.shape[0]
    channels = out.shape[1]
    half = channels // 2
    fill_ext(ext, cot, low, high)
    acc, grad = pair_products(
        lambda at: far[at : at + positions, :],
        lambda k: jnp.concatenate([k2[k], k3[k]], axis=0),
        ext,
        positions,
    )
    pooled[...] = (acc + acc1[...]).T.astype(BF16)
    lanes = doubled.shape[2]
    for j in range(channels // lanes):
        g = grad1[:, j * lanes : (j + 1) * lanes] if j * lanes < half else grad[:, j * lanes - half : (j + 1) * lanes - half]
        doubled[j, pl.ds(0, positions, 2), :] = g
        doubled[j, pl.ds(1, positions, 2), :] = g
    back = relative_order(place, rows, channels, True)
    block = 256
    for at in range(0, 2 * positions, block):
        pieces = [
            (doubled[j, at : at + block, :] * slope[at : at + block, j * lanes : (j + 1) * lanes]).astype(BF16)
            for j in range(channels // lanes)
        ]
        mixed = jnp.concatenate(pieces, axis=1)
        out[at : at + block, :] = jnp.dot(mixed, back, preferred_element_type=F32).astype(BF16)


def flip(x, bit):
    n = lax.axis_size("pos")
    return lax.ppermute(x, "pos", [(i, i ^ bit) for i in range(n)])


def on_device(activations, kernel, cotangent):
    window, channels = activations.shape
    positions, width = cotangent.shape
    rows = kernel.shape[0]
    n = lax.axis_size("pos")
    levels = n // TEAM
    quarter = channels // TEAM
    me = lax.axis_index("pos")
    place = jnp.stack([me // TEAM, me % TEAM]).astype(jnp.int32)

    cot_t = cotangent.T
    shard = kernel.transpose(1, 0, 2)

    cot_y = flip(cot_t, 2)
    shards = [shard] + [flip(shard, TEAM * m) for m in range(1, levels)]
    edge_low = jnp.concatenate([activations[-HALO:], cotangent[-HALO:]], axis=1)
    edge_high = jnp.concatenate([activations[:HALO], cotangent[:HALO]], axis=1)
    low = lax.ppermute(edge_low, "pos", [(i, i + 1) for i in range(n - 1)])
    high = lax.ppermute(edge_high, "pos", [(i + 1, i) for i in range(n - 1)])
    cot_c = flip(cot_t, 1)

    ext_rows = positions + 2 * EXT
    own, near, far = pl.pallas_call(
        functools.partial(pool_kernel, rows),
        out_shape=[
            jax.ShapeDtypeStruct((ext_rows, quarter), BF16),
            jax.ShapeDtypeStruct((ext_rows, quarter), BF16),
            jax.ShapeDtypeStruct((ext_rows, 2 * quarter), BF16),
        ],
        in_specs=[SMEM, VMEM, VMEM, VMEM],
        out_specs=[VMEM] * 3,
        compiler_params=params(32),
        name="pool",
    )(place, activations, low[:, :channels], high[:, :channels])

    far_y = flip(far, 2)
    near_c = flip(near, 1)
    cot_yc = flip(cot_y, 1)
    far_yc = flip(far_y, 1)

    split = rows % 16 == 0
    if split:
        grad_shape = [
            jax.ShapeDtypeStruct((TAPS, rows, width), F32 if m == 0 else BF16)
            for m in range(levels)
        ]
    else:
        grad_shape = [jax.ShapeDtypeStruct((TAPS, quarter, width), F32)]
    grads = pl.pallas_call(
        functools.partial(wgrad_kernel, rows),
        out_shape=grad_shape,
        in_specs=[VMEM] * 8,
        out_specs=[VMEM] * len(grad_shape),
        scratch_shapes=[pltpu.VMEM((TAPS * quarter, positions), BF16)],
        compiler_params=params(48),
        name="wgrad",
    )(own, near_c, far_y[:, :quarter], far_yc[:, quarter:], cot_t, cot_c, cot_y, cot_yc)
    if not split:
        parts = [grads[0][:, m * rows : (m + 1) * rows] for m in range(levels)]
        grads = [parts[0]] + [p.astype(BF16) for p in parts[1:]]
    total = grads[0]
    for m in range(1, levels):
        total = total + flip(grads[m], TEAM * m).astype(F32)
    kernel_grad = total.transpose(1, 0, 2)

    k0 = jnp.concatenate(shards, axis=1)
    k2 = flip(k0, 2)
    k1 = flip(k0, 1)
    k3 = flip(k2, 1)

    low_cot, high_cot = low[:, channels:], high[:, channels:]
    acc, grad, slope = pl.pallas_call(
        functools.partial(first_kernel, rows),
        out_shape=[
            jax.ShapeDtypeStruct((positions, width), F32),
            jax.ShapeDtypeStruct((positions, channels // 2), F32),
            jax.ShapeDtypeStruct((window, channels), F32),
        ],
        in_specs=[SMEM] + [VMEM] * 8,
        out_specs=[VMEM] * 3,
        scratch_shapes=[pltpu.VMEM((positions + 2 * HALO, width), BF16)],
        compiler_params=params(48),
        name="first",
    )(place, own, near, k0, k1, cotangent, low_cot, high_cot, activations)
    pooled_t, input_grad = pl.pallas_call(
        functools.partial(second_kernel, rows),
        out_shape=[
            jax.ShapeDtypeStruct((width, positions), BF16),
            jax.ShapeDtypeStruct((window, channels), BF16),
        ],
        in_specs=[SMEM] + [VMEM] * 9,
        out_specs=[VMEM] * 2,
        scratch_shapes=[
            pltpu.VMEM((positions + 2 * HALO, width), BF16),
            pltpu.VMEM((channels // 128, window, 128), F32),
        ],
        compiler_params=params(48),
        name="second",
    )(place, far, k2, k3, cotangent, low_cot, high_cot, acc, grad, slope)
    return pooled_t.T, input_grad, kernel_grad


def solution(mesh):
    placed = (P(("groups", "pos"), None), P("pos", None, None), P(("groups", "pos"), None))
    return jax.shard_map(
        on_device,
        mesh=mesh,
        in_specs=placed,
        out_specs=(
            P(("groups", "pos"), None),
            P(("groups", "pos"), None),
            P(("groups", "pos"), None, None),
        ),
        check_vma=False,
    )
```

```python
import functools

import jax
import jax.numpy as jnp
from jax import lax
from jax.experimental import pallas as pl
from jax.experimental.pallas import tpu as pltpu
from jax.sharding import PartitionSpec as P

STEP = 4
TAPS = 5
HALO = 16
TEAM = 4
EXT = 8
VMEM = pl.BlockSpec(memory_space=pltpu.VMEM)
SMEM = pl.BlockSpec(memory_space=pltpu.SMEM)
F32 = jnp.float32
BF16 = jnp.bfloat16


def params(mib):
    return pltpu.CompilerParams(vmem_limit_bytes=mib * 2**20)


def gelu_value(v):
    return 0.5 * v * (1.0 + lax.erf(v * 0.7071067811865476))


def gelu_slope(v):
    return (
        0.5 * (1.0 + lax.erf(v * 0.7071067811865476))
        + v * jnp.exp(-0.5 * v * v) * 0.3989422804014327
    )


def relative_order(place, rows, channels, transposed):
    shape = (channels, channels)
    chan = lax.broadcasted_iota(jnp.int32, shape, 1 if transposed else 0)
    col = lax.broadcasted_iota(jnp.int32, shape, 0 if transposed else 1)
    quarter = channels // TEAM
    mate = lax.div(col, quarter)
    within = lax.rem(col, quarter)
    slot = lax.div(within, rows)
    row = lax.rem(within, rows)
    level = jnp.zeros_like(slot)
    bit = quarter // rows // 2
    while bit:
        level = level * 2 + lax.rem(slot, 2)
        slot = lax.div(slot, 2)
        bit //= 2
    want = rows * (TEAM * (level ^ place[0]) + (mate ^ place[1])) + row
    return jnp.where(chan == want, 1.0, 0.0).astype(BF16)


def pool_kernel(rows, place, act, low, high, *mates):
    channels = act.shape[1]
    quarter = channels // TEAM
    order = relative_order(place, rows, channels, False)

    def pooled(g):
        t = g.shape[0]
        u = lax.broadcasted_iota(jnp.int32, (t // 2, t), 0)
        v = lax.broadcasted_iota(jnp.int32, (t // 2, t), 1)
        halves = jnp.where(lax.div(v, 2) == u, 0.5, 0.0).astype(BF16)
        s = jnp.dot(halves, g, preferred_element_type=F32).astype(BF16)
        return jnp.dot(s, order, preferred_element_type=F32).astype(BF16)

    def put(at, s):
        n = s.shape[0]
        for r, mate in enumerate(mates):
            mate[at : at + n, :] = s[:, r * quarter : (r + 1) * quarter]

    def gelu(v):
        return gelu_value(v.astype(F32)).astype(BF16)

    window = act.shape[0]
    block = 256
    g_prev = gelu(low[...])
    for at in range(0, window, block):
        g = gelu(act[at : at + block, :])
        joined = jnp.concatenate([g_prev, g[: block - HALO]], axis=0)
        put(at // 2, pooled(joined))
        g_prev = g[block - HALO :]
    put(window // 2, pooled(jnp.concatenate([g_prev, gelu(high[...])], axis=0)))


def wgrad_kernel(rows, s0, s1, s2, s3, c0, c1, c2, c3, *refs):
    *outs, left = refs
    positions = c0.shape[1]
    quarter = s0.shape[1]
    total = None
    for s, c in ((s0, c0), (s1, c1), (s2, c2), (s3, c3)):
        for k in range(TAPS):
            at = EXT + 2 * (k - 2)
            left[k * quarter : (k + 1) * quarter, :] = s[at : at + positions, :].T
        term = lax.dot_general(
            left[...], c[...], (((1,), (1,)), ((), ())), preferred_element_type=F32
        )
        total = term if total is None else total + term
    if len(outs) == 1:
        for k in range(TAPS):
            outs[0][k] = total[k * quarter : (k + 1) * quarter]
    else:
        for k in range(TAPS):
            for m, out in enumerate(outs):
                size = out.shape[1]
                at = k * quarter + m * size
                out[k] = total[at : at + size].astype(out.dtype)


def fill_ext(ext, cot, low, high):
    positions = cot.shape[0]
    ext[:HALO, :] = low[...]
    ext[HALO : HALO + positions, :] = cot[...]
    ext[HALO + positions :, :] = high[...]


def pair_products(s_pair, k_pair, ext, positions):
    acc = None
    grad = None
    for k in range(TAPS):
        at = EXT + 2 * (k - 2)
        weights = k_pair(k)
        term = jnp.dot(s_pair(at), weights, preferred_element_type=F32)
        acc = term if acc is None else acc + term
        back = HALO - 2 * (k - 2)
        term = lax.dot_general(
            ext[back : back + positions, :],
            weights,
            (((1,), (1,)), ((), ())),
            preferred_element_type=F32,
        )
        grad = term if grad is None else grad + term
    return acc, grad


def first_kernel(rows, place, s0, s1, k0, k1, cot, low, high, act, acc, grad, slope, ext):
    positions = cot.shape[0]
    fill_ext(ext, cot, low, high)
    acc[...], grad[...] = pair_products(
        lambda at: jnp.concatenate([s0[at : at + positions], s1[at : at + positions]], axis=1),
        lambda k: jnp.concatenate([k0[k], k1[k]], axis=0)[:, : cot.shape[1]],
        ext,
        positions,
    )
    order = relative_order(place, rows, act.shape[1], False)
    block = 256
    for at in range(0, act.shape[0], block):
        v = jnp.dot(act[at : at + block, :], order, preferred_element_type=F32)
        slope[at : at + block, :] = 0.5 * gelu_slope(v)


def second_kernel(
    rows, place, s2, s3, k2, k3, cot, low, high, acc1, grad1, slope, pooled, out, ext, doubled
):
    positions = cot.shape[0]
    channels = out.shape[1]
    half = channels // 2
    fill_ext(ext, cot, low, high)
    acc, grad = pair_products(
        lambda at: jnp.concatenate([s2[at : at + positions], s3[at : at + positions]], axis=1),
        lambda k: jnp.concatenate([k2[k], k3[k]], axis=0)[:, : cot.shape[1]],
        ext,
        positions,
    )
    pooled[...] = (acc + acc1[...]).T.astype(BF16)
    lanes = doubled.shape[2]
    for j in range(channels // lanes):
        g = grad1[:, j * lanes : (j + 1) * lanes] if j * lanes < half else grad[:, j * lanes - half : (j + 1) * lanes - half]
        doubled[j, pl.ds(0, positions, 2), :] = g
        doubled[j, pl.ds(1, positions, 2), :] = g
    back = relative_order(place, rows, channels, True)
    block = 256
    for at in range(0, 2 * positions, block):
        pieces = [
            (doubled[j, at : at + block, :] * slope[at : at + block, j * lanes : (j + 1) * lanes]).astype(BF16)
            for j in range(channels // lanes)
        ]
        mixed = jnp.concatenate(pieces, axis=1)
        out[at : at + block, :] = jnp.dot(mixed, back, preferred_element_type=F32).astype(BF16)


def after(x, *first):
    return lax.optimization_barrier((x, first))[0]


def flip(x, bit):
    n = lax.axis_size("pos")
    return lax.ppermute(x, "pos", [(i, i ^ bit) for i in range(n)])


def on_device(activations, kernel, cotangent):
    window, channels = activations.shape
    positions, width = cotangent.shape
    rows = kernel.shape[0]
    n = lax.axis_size("pos")
    levels = n // TEAM
    quarter = channels // TEAM
    me = lax.axis_index("pos")
    place = jnp.stack([me // TEAM, me % TEAM]).astype(jnp.int32)

    cot_t = cotangent.T
    shard = kernel.transpose(1, 0, 2)

    cot_y = flip(cot_t, 2)
    head = levels // 2
    first_block = flip(shard, TEAM * head) if head else None
    edge_low = jnp.concatenate([activations[-HALO:], cotangent[-HALO:]], axis=1)
    edge_high = jnp.concatenate([activations[:HALO], cotangent[:HALO]], axis=1)
    low = lax.ppermute(edge_low, "pos", [(i, i + 1) for i in range(n - 1)])
    high = lax.ppermute(edge_high, "pos", [(i + 1, i) for i in range(n - 1)])
    cot_c = flip(cot_t, 1)

    ext_rows = positions + 2 * EXT
    pieces = pl.pallas_call(
        functools.partial(pool_kernel, rows),
        out_shape=[jax.ShapeDtypeStruct((ext_rows, quarter), BF16)] * TEAM,
        in_specs=[SMEM, VMEM, VMEM, VMEM],
        out_specs=[VMEM] * TEAM,
        cost_estimate=pl.CostEstimate(flops=1, bytes_accessed=1, transcendentals=0),
        compiler_params=params(32),
        name="pool",
    )(place, activations, low[:, :channels], high[:, :channels])

    order = [0]
    k0 = shard
    while len(order) < levels:
        bit = levels // 2 // len(order)
        got = after(first_block, pieces) if bit == head else flip(k0, TEAM * bit)
        k0 = jnp.concatenate([k0, got], axis=1)
        order += [m ^ bit for m in order]
    far = after(pieces[2:], cot_y)
    mates = [pieces[0], flip(pieces[1], 1), flip(far[0], 2), flip(far[1], 3)]
    cot_y = after(cot_y, mates[1])
    cot_yc = flip(cot_y, 1)

    halves = max(levels // 2, 1)
    split = rows % 16 == 0
    if split:
        grad_shape = [
            jax.ShapeDtypeStruct((TAPS, halves * rows, width), dtype) for dtype in (F32, BF16)
        ]
    else:
        grad_shape = [jax.ShapeDtypeStruct((TAPS, quarter, width), F32)]
    grads = pl.pallas_call(
        functools.partial(wgrad_kernel, rows),
        out_shape=grad_shape,
        in_specs=[VMEM] * 8,
        out_specs=[VMEM] * len(grad_shape),
        scratch_shapes=[pltpu.VMEM((TAPS * quarter, positions), BF16)],
        cost_estimate=pl.CostEstimate(flops=1, bytes_accessed=1, transcendentals=0),
        compiler_params=params(48),
        name="wgrad",
    )(*mates, cot_t, cot_c, cot_y, cot_yc)
    keep = grads[0] if split else grads[0][:, : halves * rows]
    give = grads[1] if split else grads[0][:, halves * rows :].astype(BF16)
    bits = []
    bit = 1
    while bit < levels:
        bits.append(bit)
        bit *= 2
    last = None
    for i, bit in enumerate(bits):
        got = flip(give, TEAM * bit)
        if i + 1 == len(bits):
            last = (keep, got)
            break
        keep = keep + got.astype(F32)
        half = keep.shape[1] // 2
        keep, give = keep[:, :half], keep[:, half:].astype(BF16)

    k0 = after(k0, mates)
    k0 = jnp.pad(k0, ((0, 0), (0, 0), (0, -width % 128)))
    k2 = flip(k0, 2)
    k1 = flip(k0, 1)

    low_cot, high_cot = low[:, channels:], high[:, channels:]
    acc, grad, slope = pl.pallas_call(
        functools.partial(first_kernel, rows),
        out_shape=[
            jax.ShapeDtypeStruct((positions, width), F32),
            jax.ShapeDtypeStruct((positions, channels // 2), F32),
            jax.ShapeDtypeStruct((window, channels), F32),
        ],
        in_specs=[SMEM] + [VMEM] * 8,
        out_specs=[VMEM] * 3,
        scratch_shapes=[pltpu.VMEM((positions + 2 * HALO, width), BF16)],
        cost_estimate=pl.CostEstimate(flops=1, bytes_accessed=1, transcendentals=0),
        compiler_params=params(48),
        name="first",
    )(place, pieces[0], pieces[1], k0, k1, cotangent, low_cot, high_cot, activations)
    k2 = after(k2, acc, keep)
    k3 = flip(k2, 1)
    pooled_t, input_grad = pl.pallas_call(
        functools.partial(second_kernel, rows),
        out_shape=[
            jax.ShapeDtypeStruct((width, positions), BF16),
            jax.ShapeDtypeStruct((window, channels), BF16),
        ],
        in_specs=[SMEM] + [VMEM] * 10,
        out_specs=[VMEM] * 2,
        scratch_shapes=[
            pltpu.VMEM((positions + 2 * HALO, width), BF16),
            pltpu.VMEM((channels // 128, window, 128), F32),
        ],
        cost_estimate=pl.CostEstimate(flops=1, bytes_accessed=1, transcendentals=0),
        compiler_params=params(48),
        name="second",
    )(place, pieces[2], pieces[3], k2, k3, cotangent, low_cot, high_cot, acc, grad, slope)
    if last is not None:
        keep, got = last[0], after(last[1], pooled_t)
        keep = keep + got.astype(F32)
    return pooled_t.T, input_grad, keep.transpose(1, 0, 2)


def solution(mesh):
    placed = (P(("groups", "pos"), None), P("pos", None, None), P(("groups", "pos"), None))
    return jax.shard_map(
        on_device,
        mesh=mesh,
        in_specs=placed,
        out_specs=(
            P(("groups", "pos"), None),
            P(("groups", "pos"), None),
            P(("groups", "pos"), None, None),
        ),
        check_vma=False,
    )
```

```python
import functools

import jax
import jax.numpy as jnp
from jax import lax
from jax.experimental import pallas as pl
from jax.experimental.pallas import tpu as pltpu
from jax.sharding import PartitionSpec as P

STEP = 4
TAPS = 5
HALO = 16
TEAM = 4
EXT = 8
VMEM = pl.BlockSpec(memory_space=pltpu.VMEM)
SMEM = pl.BlockSpec(memory_space=pltpu.SMEM)
F32 = jnp.float32
BF16 = jnp.bfloat16


def params(mib):
    return pltpu.CompilerParams(vmem_limit_bytes=mib * 2**20)


def gelu_value(v):
    return 0.5 * v * (1.0 + lax.erf(v * 0.7071067811865476))


def gelu_slope(v):
    return (
        0.5 * (1.0 + lax.erf(v * 0.7071067811865476))
        + v * jnp.exp(-0.5 * v * v) * 0.3989422804014327
    )


def relative_order(place, rows, channels, transposed):
    shape = (channels, channels)
    chan = lax.broadcasted_iota(jnp.int32, shape, 1 if transposed else 0)
    col = lax.broadcasted_iota(jnp.int32, shape, 0 if transposed else 1)
    quarter = channels // TEAM
    mate = lax.div(col, quarter)
    within = lax.rem(col, quarter)
    slot = lax.div(within, rows)
    row = lax.rem(within, rows)
    level = jnp.zeros_like(slot)
    bit = quarter // rows // 2
    while bit:
        level = level * 2 + lax.rem(slot, 2)
        slot = lax.div(slot, 2)
        bit //= 2
    want = rows * (TEAM * (level ^ place[0]) + (mate ^ place[1])) + row
    return jnp.where(chan == want, 1.0, 0.0).astype(BF16)


def pool_kernel(rows, place, act, low, high, *mates):
    channels = act.shape[1]
    quarter = channels // TEAM
    order = relative_order(place, rows, channels, False)

    def pooled(g):
        t = g.shape[0]
        u = lax.broadcasted_iota(jnp.int32, (t // 2, t), 0)
        v = lax.broadcasted_iota(jnp.int32, (t // 2, t), 1)
        halves = jnp.where(lax.div(v, 2) == u, 0.5, 0.0).astype(BF16)
        s = jnp.dot(halves, g, preferred_element_type=F32).astype(BF16)
        return jnp.dot(s, order, preferred_element_type=F32).astype(BF16)

    def put(at, s):
        n = s.shape[0]
        for r, mate in enumerate(mates):
            mate[at : at + n, :] = s[:, r * quarter : (r + 1) * quarter]

    def gelu(v):
        return gelu_value(v.astype(F32)).astype(BF16)

    window = act.shape[0]
    block = 256
    g_prev = gelu(low[...])
    for at in range(0, window, block):
        g = gelu(act[at : at + block, :])
        joined = jnp.concatenate([g_prev, g[: block - HALO]], axis=0)
        put(at // 2, pooled(joined))
        g_prev = g[block - HALO :]
    put(window // 2, pooled(jnp.concatenate([g_prev, gelu(high[...])], axis=0)))


def wgrad_kernel(rows, s0, s1, s2, s3, c0, c1, c2, c3, *refs):
    *outs, left = refs
    positions = c0.shape[1]
    quarter = s0.shape[1]
    total = None
    for s, c in ((s0, c0), (s1, c1), (s2, c2), (s3, c3)):
        for k in range(TAPS):
            at = EXT + 2 * (k - 2)
            left[k * quarter : (k + 1) * quarter, :] = s[at : at + positions, :].T
        term = lax.dot_general(
            left[...], c[...], (((1,), (1,)), ((), ())), preferred_element_type=F32
        )
        total = term if total is None else total + term
    if len(outs) == 1:
        for k in range(TAPS):
            outs[0][k] = total[k * quarter : (k + 1) * quarter]
    else:
        for k in range(TAPS):
            for m, out in enumerate(outs):
                size = out.shape[1]
                at = k * quarter + m * size
                out[k] = total[at : at + size].astype(out.dtype)


def fill_ext(ext, cot, low, high):
    positions = cot.shape[0]
    ext[:HALO, :] = low[...]
    ext[HALO : HALO + positions, :] = cot[...]
    ext[HALO + positions :, :] = high[...]


def pair_products(s_pair, k_pair, ext, positions):
    acc = None
    grad = None
    for k in range(TAPS):
        at = EXT + 2 * (k - 2)
        weights = k_pair(k)
        term = jnp.dot(s_pair(at), weights, preferred_element_type=F32)
        acc = term if acc is None else acc + term
        back = HALO - 2 * (k - 2)
        term = lax.dot_general(
            ext[back : back + positions, :],
            weights,
            (((1,), (1,)), ((), ())),
            preferred_element_type=F32,
        )
        grad = term if grad is None else grad + term
    return acc, grad


def first_kernel(rows, place, s0, s1, k0, k1, cot, low, high, act, acc, grad, slope, ext):
    positions = cot.shape[0]
    fill_ext(ext, cot, low, high)
    acc[...], grad[...] = pair_products(
        lambda at: jnp.concatenate([s0[at : at + positions], s1[at : at + positions]], axis=1),
        lambda k: jnp.concatenate([k0[k], k1[k]], axis=0)[:, : cot.shape[1]],
        ext,
        positions,
    )
    order = relative_order(place, rows, act.shape[1], False)
    block = 256
    for at in range(0, act.shape[0], block):
        v = jnp.dot(act[at : at + block, :], order, preferred_element_type=F32)
        slope[at : at + block, :] = 0.5 * gelu_slope(v)


def second_kernel(
    rows, place, s2, s3, k2, k3, cot, low, high, acc1, grad1, slope, pooled, out, ext, doubled
):
    positions = cot.shape[0]
    channels = out.shape[1]
    half = channels // 2
    fill_ext(ext, cot, low, high)
    acc, grad = pair_products(
        lambda at: jnp.concatenate([s2[at : at + positions], s3[at : at + positions]], axis=1),
        lambda k: jnp.concatenate([k2[k], k3[k]], axis=0)[:, : cot.shape[1]],
        ext,
        positions,
    )
    pooled[...] = (acc + acc1[...]).T.astype(BF16)
    lanes = doubled.shape[2]
    for j in range(channels // lanes):
        g = grad1[:, j * lanes : (j + 1) * lanes] if j * lanes < half else grad[:, j * lanes - half : (j + 1) * lanes - half]
        doubled[j, pl.ds(0, positions, 2), :] = g
        doubled[j, pl.ds(1, positions, 2), :] = g
    back = relative_order(place, rows, channels, True)
    block = 256
    for at in range(0, 2 * positions, block):
        pieces = [
            (doubled[j, at : at + block, :] * slope[at : at + block, j * lanes : (j + 1) * lanes]).astype(BF16)
            for j in range(channels // lanes)
        ]
        mixed = jnp.concatenate(pieces, axis=1)
        out[at : at + block, :] = jnp.dot(mixed, back, preferred_element_type=F32).astype(BF16)


def after(x, *first):
    return lax.optimization_barrier((x, first))[0]


def flip(x, bit):
    n = lax.axis_size("pos")
    return lax.ppermute(x, "pos", [(i, i ^ bit) for i in range(n)])


def on_device(activations, kernel, cotangent):
    window, channels = activations.shape
    positions, width = cotangent.shape
    rows = kernel.shape[0]
    n = lax.axis_size("pos")
    levels = n // TEAM
    quarter = channels // TEAM
    me = lax.axis_index("pos")
    place = jnp.stack([me // TEAM, me % TEAM]).astype(jnp.int32)

    cot_t = cotangent.T
    shard = kernel.transpose(1, 0, 2)

    cot_y = flip(cot_t, 2)
    order = [0]
    blocks = [shard]
    while len(order) < levels:
        bit = levels // 2 // len(order)
        blocks = blocks + [flip(block, TEAM * bit) for block in blocks]
        order += [m ^ bit for m in order]
    k0 = jnp.concatenate(blocks, axis=1)
    early = blocks[1:2] + blocks[levels // 2 : levels // 2 + 1]
    edge_low = jnp.concatenate([activations[-HALO:], cotangent[-HALO:]], axis=1)
    edge_high = jnp.concatenate([activations[:HALO], cotangent[:HALO]], axis=1)
    low = lax.ppermute(edge_low, "pos", [(i, i + 1) for i in range(n - 1)])
    high = lax.ppermute(edge_high, "pos", [(i + 1, i) for i in range(n - 1)])
    cot_c = flip(cot_t, 1)

    ext_rows = positions + 2 * EXT
    pieces = pl.pallas_call(
        functools.partial(pool_kernel, rows),
        out_shape=[jax.ShapeDtypeStruct((ext_rows, quarter), BF16)] * TEAM,
        in_specs=[SMEM, VMEM, VMEM, VMEM],
        out_specs=[VMEM] * TEAM,
        compiler_params=params(32),
        name="pool",
    )(place, after(activations, *early), low[:, :channels], high[:, :channels])

    far = after(pieces[2:], cot_y)
    mates = [pieces[0], flip(pieces[1], 1), flip(far[0], 2), flip(far[1], 3)]
    cot_y = after(cot_y, mates[1])
    cot_yc = flip(cot_y, 1)

    split = rows % 16 == 0
    if split:
        grad_shape = [
            jax.ShapeDtypeStruct((TAPS, rows, width), BF16 if m else F32) for m in range(levels)
        ]
    else:
        grad_shape = [jax.ShapeDtypeStruct((TAPS, quarter, width), F32)]
    grads = pl.pallas_call(
        functools.partial(wgrad_kernel, rows),
        out_shape=grad_shape,
        in_specs=[VMEM] * 8,
        out_specs=[VMEM] * len(grad_shape),
        scratch_shapes=[pltpu.VMEM((TAPS * quarter, positions), BF16)],
        compiler_params=params(48),
        name="wgrad",
    )(*mates, cot_t, cot_c, cot_y, cot_yc)
    if not split:
        parts = [grads[0][:, m * rows : (m + 1) * rows] for m in range(levels)]
        grads = parts[:1] + [p.astype(BF16) for p in parts[1:]]
    terms = [flip(g, TEAM * m) for g, m in zip(grads[1:], order[1:])]

    k0 = after(k0, mates, cot_c, cot_yc)
    k0 = jnp.pad(k0, ((0, 0), (0, 0), (0, -width % 128)))
    k2 = flip(k0, 2)
    k1 = flip(k0, 1)

    low_cot, high_cot = low[:, channels:], high[:, channels:]
    acc, grad, slope = pl.pallas_call(
        functools.partial(first_kernel, rows),
        out_shape=[
            jax.ShapeDtypeStruct((positions, width), F32),
            jax.ShapeDtypeStruct((positions, channels // 2), F32),
            jax.ShapeDtypeStruct((window, channels), F32),
        ],
        in_specs=[SMEM] + [VMEM] * 8,
        out_specs=[VMEM] * 3,
        scratch_shapes=[pltpu.VMEM((positions + 2 * HALO, width), BF16)],
        compiler_params=params(48),
        name="first",
    )(place, pieces[0], pieces[1], k0, k1, cotangent, low_cot, high_cot, activations)
    k2 = after(k2, acc, terms)
    k3 = flip(k2, 1)
    pooled_t, input_grad = pl.pallas_call(
        functools.partial(second_kernel, rows),
        out_shape=[
            jax.ShapeDtypeStruct((width, positions), BF16),
            jax.ShapeDtypeStruct((window, channels), BF16),
        ],
        in_specs=[SMEM] + [VMEM] * 10,
        out_specs=[VMEM] * 2,
        scratch_shapes=[
            pltpu.VMEM((positions + 2 * HALO, width), BF16),
            pltpu.VMEM((channels // 128, window, 128), F32),
        ],
        compiler_params=params(48),
        name="second",
    )(place, pieces[2], pieces[3], k2, k3, cotangent, low_cot, high_cot, acc, grad, slope)
    total = grads[0]
    for term in terms:
        total = total + term.astype(F32)
    return pooled_t.T, input_grad, total.transpose(1, 0, 2)


def solution(mesh):
    placed = (P(("groups", "pos"), None), P("pos", None, None), P(("groups", "pos"), None))
    return jax.shard_map(
        on_device,
        mesh=mesh,
        in_specs=placed,
        out_specs=(
            P(("groups", "pos"), None),
            P(("groups", "pos"), None),
            P(("groups", "pos"), None, None),
        ),
        check_vma=False,
    )
```

```python
import functools

import jax
import jax.numpy as jnp
from jax import lax
from jax.experimental import pallas as pl
from jax.experimental.pallas import tpu as pltpu
from jax.sharding import PartitionSpec as P

STEP = 4
TAPS = 5
HALO = 16
TEAM = 4
EXT = 8
VMEM = pl.BlockSpec(memory_space=pltpu.VMEM)
SMEM = pl.BlockSpec(memory_space=pltpu.SMEM)
F32 = jnp.float32
BF16 = jnp.bfloat16


def params(mib):
    return pltpu.CompilerParams(vmem_limit_bytes=mib * 2**20)


def gelu_value(v):
    return 0.5 * v * (1.0 + lax.erf(v * 0.7071067811865476))


def gelu_slope(v):
    return (
        0.5 * (1.0 + lax.erf(v * 0.7071067811865476))
        + v * jnp.exp(-0.5 * v * v) * 0.3989422804014327
    )


def relative_order(place, rows, channels, transposed):
    shape = (channels, channels)
    chan = lax.broadcasted_iota(jnp.int32, shape, 1 if transposed else 0)
    col = lax.broadcasted_iota(jnp.int32, shape, 0 if transposed else 1)
    quarter = channels // TEAM
    mate = lax.div(col, quarter)
    within = lax.rem(col, quarter)
    slot = lax.div(within, rows)
    row = lax.rem(within, rows)
    level = jnp.zeros_like(slot)
    bit = quarter // rows // 2
    while bit:
        level = level * 2 + lax.rem(slot, 2)
        slot = lax.div(slot, 2)
        bit //= 2
    want = rows * (TEAM * (level ^ place[0]) + (mate ^ place[1])) + row
    return jnp.where(chan == want, 1.0, 0.0).astype(BF16)


def pool_kernel(rows, place, act, low, high, *mates):
    channels = act.shape[1]
    quarter = channels // TEAM
    order = relative_order(place, rows, channels, False)

    def pooled(g):
        t = g.shape[0]
        u = lax.broadcasted_iota(jnp.int32, (t // 2, t), 0)
        v = lax.broadcasted_iota(jnp.int32, (t // 2, t), 1)
        halves = jnp.where(lax.div(v, 2) == u, 0.5, 0.0).astype(BF16)
        s = jnp.dot(halves, g, preferred_element_type=F32).astype(BF16)
        return jnp.dot(s, order, preferred_element_type=F32).astype(BF16)

    def put(at, s):
        n = s.shape[0]
        for r, mate in enumerate(mates):
            mate[at : at + n, :] = s[:, r * quarter : (r + 1) * quarter]

    def gelu(v):
        return gelu_value(v.astype(F32)).astype(BF16)

    window = act.shape[0]
    block = 256
    g_prev = gelu(low[...])
    for at in range(0, window, block):
        g = gelu(act[at : at + block, :])
        joined = jnp.concatenate([g_prev, g[: block - HALO]], axis=0)
        put(at // 2, pooled(joined))
        g_prev = g[block - HALO :]
    put(window // 2, pooled(jnp.concatenate([g_prev, gelu(high[...])], axis=0)))


def wgrad_kernel(rows, s0, s1, s2, s3, c0, c1, c2, c3, *refs):
    *outs, left = refs
    positions = c0.shape[1]
    quarter = s0.shape[1]
    total = None
    for s, c in ((s0, c0), (s1, c1), (s2, c2), (s3, c3)):
        for k in range(TAPS):
            at = EXT + 2 * (k - 2)
            left[k * quarter : (k + 1) * quarter, :] = s[at : at + positions, :].T
        term = lax.dot_general(
            left[...], c[...], (((1,), (1,)), ((), ())), preferred_element_type=F32
        )
        total = term if total is None else total + term
    if len(outs) == 1:
        for k in range(TAPS):
            outs[0][k] = total[k * quarter : (k + 1) * quarter]
    else:
        for k in range(TAPS):
            for m, out in enumerate(outs):
                size = out.shape[1]
                at = k * quarter + m * size
                out[k] = total[at : at + size].astype(out.dtype)


def fill_ext(ext, cot, low, high):
    positions = cot.shape[0]
    ext[:HALO, :] = low[...]
    ext[HALO : HALO + positions, :] = cot[...]
    ext[HALO + positions :, :] = high[...]


def taps_of(k_a, k_b, width):
    return [jnp.concatenate([k_a[k], k_b[k]], axis=0)[:, :width] for k in range(TAPS)]


def products(columns, shifted, weights):
    acc = jnp.dot(columns, jnp.concatenate(weights, axis=0), preferred_element_type=F32)
    grad = None
    for k, weight in enumerate(weights):
        term = lax.dot_general(
            shifted[k], weight, (((1,), (1,)), ((), ())), preferred_element_type=F32
        )
        grad = term if grad is None else grad + term
    return acc, grad


def fill_columns(columns, s_a, s_b, positions):
    quarter = s_a.shape[1]
    for k in range(TAPS):
        at = EXT + 2 * (k - 2)
        for i, s in enumerate((s_a, s_b)):
            lane = (2 * k + i) * quarter
            columns[:, lane : lane + quarter] = s[at : at + positions, :]


def spread(grad, slope, doubled, back, base, out):
    positions = grad.shape[0]
    blocks, _, lanes = doubled.shape
    for j in range(blocks):
        g = grad[:, j * lanes : (j + 1) * lanes]
        doubled[j, pl.ds(0, positions, 2), :] = g
        doubled[j, pl.ds(1, positions, 2), :] = g
    block = 256
    for at in range(0, 2 * positions, block):
        rows = slice(at, at + block)
        mixed = jnp.concatenate(
            [
                (doubled[j, rows, :] * slope(rows, j * lanes, (j + 1) * lanes)).astype(BF16)
                for j in range(blocks)
            ],
            axis=1,
        )
        put = jnp.dot(mixed, back, preferred_element_type=F32)
        if base is not None:
            put = put + base[rows, :].astype(F32)
        out[rows, :] = put.astype(BF16)


def first_kernel(rows, place, s0, s1, s2, s3, k0, k1, cot, low, high, act, *refs):
    acc, part, slope, back, later, shifted, ext, columns, doubled = refs
    positions, width = cot.shape
    window, channels = act.shape
    half = channels // 2
    fill_ext(ext, cot, low, high)
    for k in range(TAPS):
        at = HALO - 2 * (k - 2)
        shifted[k] = ext[at : at + positions, :]
    fill_columns(columns, s0, s1, positions)
    fill_columns(later, s2, s3, positions)
    order = relative_order(place, rows, channels, True)
    back[...] = order[half:, :]
    acc[...], grad = products(columns[...], shifted, taps_of(k0, k1, width))

    def slope_of(rows, start, stop):
        v = lax.dot_general(
            act[rows, :], order[start:stop, :], (((1,), (1,)), ((), ())), preferred_element_type=F32
        )
        return 0.5 * gelu_slope(v)

    spread(grad, slope_of, doubled, order[:half, :], None, part)
    for at in range(0, window, 256):
        slope[at : at + 256, :] = slope_of(slice(at, at + 256), half, channels)


def second_kernel(k2, k3, columns, shifted, acc1, part, slope, back, pooled, out, doubled):
    acc, grad = products(columns[...], shifted, taps_of(k2, k3, shifted.shape[2]))
    pooled[...] = (acc + acc1[...]).astype(BF16).T
    spread(grad, lambda rows, i, j: slope[rows, i:j], doubled, back[...], part, out)


def after(x, *first):
    return lax.optimization_barrier((x, first))[0]


def flip(x, bit):
    n = lax.axis_size("pos")
    return lax.ppermute(x, "pos", [(i, i ^ bit) for i in range(n)])


def on_device(activations, kernel, cotangent):
    window, channels = activations.shape
    positions, width = cotangent.shape
    rows = kernel.shape[0]
    n = lax.axis_size("pos")
    levels = n // TEAM
    quarter = channels // TEAM
    me = lax.axis_index("pos")
    place = jnp.stack([me // TEAM, me % TEAM]).astype(jnp.int32)

    cot_t = cotangent.T
    shard = kernel.transpose(1, 0, 2)

    cot_y = flip(cot_t, 2)
    order = [0]
    blocks = [shard]
    while len(order) < levels:
        bit = levels // 2 // len(order)
        blocks = blocks + [flip(block, TEAM * bit) for block in blocks]
        order += [m ^ bit for m in order]
    k0 = jnp.concatenate(blocks, axis=1)
    early = blocks[1:2] + blocks[levels // 2 : levels // 2 + 1]
    edge_low = jnp.concatenate([activations[-HALO:], cotangent[-HALO:]], axis=1)
    edge_high = jnp.concatenate([activations[:HALO], cotangent[:HALO]], axis=1)
    low = lax.ppermute(edge_low, "pos", [(i, i + 1) for i in range(n - 1)])
    high = lax.ppermute(edge_high, "pos", [(i + 1, i) for i in range(n - 1)])
    cot_c = flip(cot_t, 1)

    ext_rows = positions + 2 * EXT
    pieces = pl.pallas_call(
        functools.partial(pool_kernel, rows),
        out_shape=[jax.ShapeDtypeStruct((ext_rows, quarter), BF16)] * TEAM,
        in_specs=[SMEM, VMEM, VMEM, VMEM],
        out_specs=[VMEM] * TEAM,
        compiler_params=params(32),
        name="pool",
    )(place, after(activations, *early), low[:, :channels], high[:, :channels])

    far = after(pieces[2:], cot_y)
    mates = [pieces[0], flip(pieces[1], 1), flip(far[0], 2), flip(far[1], 3)]
    cot_y = after(cot_y, mates[1])
    cot_yc = flip(cot_y, 1)

    split = rows % 16 == 0
    if split:
        grad_shape = [
            jax.ShapeDtypeStruct((TAPS, rows, width), BF16 if m else F32) for m in range(levels)
        ]
    else:
        grad_shape = [jax.ShapeDtypeStruct((TAPS, quarter, width), F32)]
    grads = pl.pallas_call(
        functools.partial(wgrad_kernel, rows),
        out_shape=grad_shape,
        in_specs=[VMEM] * 8,
        out_specs=[VMEM] * len(grad_shape),
        scratch_shapes=[pltpu.VMEM((TAPS * quarter, positions), BF16)],
        compiler_params=params(48),
        name="wgrad",
    )(*mates, cot_t, cot_c, cot_y, cot_yc)
    if not split:
        parts = [grads[0][:, m * rows : (m + 1) * rows] for m in range(levels)]
        grads = parts[:1] + [p.astype(BF16) for p in parts[1:]]
    terms = [flip(g, TEAM * m) for g, m in zip(grads[1:], order[1:])]

    k0 = after(k0, mates, cot_c, cot_yc)
    k0 = jnp.pad(k0, ((0, 0), (0, 0), (0, -width % 128)))
    k2 = flip(k0, 2)
    k1 = flip(k0, 1)

    low_cot, high_cot = low[:, channels:], high[:, channels:]
    half = channels // 2
    doubled = pltpu.VMEM((half // 128, window, 128), F32)
    acc, part, *handed = pl.pallas_call(
        functools.partial(first_kernel, rows),
        out_shape=[
            jax.ShapeDtypeStruct((positions, width), F32),
            jax.ShapeDtypeStruct((window, channels), BF16),
            jax.ShapeDtypeStruct((window, half), F32),
            jax.ShapeDtypeStruct((half, channels), BF16),
            jax.ShapeDtypeStruct((positions, TAPS * half), BF16),
            jax.ShapeDtypeStruct((TAPS, positions, width), BF16),
        ],
        in_specs=[SMEM] + [VMEM] * 10,
        out_specs=[VMEM] * 6,
        scratch_shapes=[
            pltpu.VMEM((positions + 2 * HALO, width), BF16),
            pltpu.VMEM((positions, TAPS * half), BF16),
            doubled,
        ],
        compiler_params=params(40),
        name="first",
    )(place, *pieces, k0, k1, cotangent, low_cot, high_cot, activations)
    slope, back, columns, shifted = handed
    k2 = after(k2, acc, terms)
    k3 = flip(k2, 1)
    pooled_t, input_grad = pl.pallas_call(
        second_kernel,
        out_shape=[
            jax.ShapeDtypeStruct((width, positions), BF16),
            jax.ShapeDtypeStruct((window, channels), BF16),
        ],
        in_specs=[VMEM] * 8,
        out_specs=[VMEM] * 2,
        scratch_shapes=[doubled],
        compiler_params=params(40),
        name="second",
    )(k2, k3, columns, shifted, acc, part, slope, back)
    total = grads[0]
    for term in terms:
        total = total + term.astype(F32)
    return pooled_t.T, input_grad, total.transpose(1, 0, 2)


def solution(mesh):
    placed = (P(("groups", "pos"), None), P("pos", None, None), P(("groups", "pos"), None))
    return jax.shard_map(
        on_device,
        mesh=mesh,
        in_specs=placed,
        out_specs=(
            P(("groups", "pos"), None),
            P(("groups", "pos"), None),
            P(("groups", "pos"), None, None),
        ),
        check_vma=False,
    )
```

```python
import functools

import jax
import jax.numpy as jnp
from jax import lax
from jax.experimental import pallas as pl
from jax.experimental.pallas import tpu as pltpu
from jax.sharding import PartitionSpec as P

STEP = 4
TAPS = 5
HALO = 16
TEAM = 4
EXT = 8
VMEM = pl.BlockSpec(memory_space=pltpu.VMEM)
SMEM = pl.BlockSpec(memory_space=pltpu.SMEM)
F32 = jnp.float32
BF16 = jnp.bfloat16


def params(mib):
    return pltpu.CompilerParams(vmem_limit_bytes=mib * 2**20)


def gelu_value(v):
    return 0.5 * v * (1.0 + lax.erf(v * 0.7071067811865476))


def gelu_slope(v):
    return (
        0.5 * (1.0 + lax.erf(v * 0.7071067811865476))
        + v * jnp.exp(-0.5 * v * v) * 0.3989422804014327
    )


def relative_order(place, rows, channels, transposed):
    shape = (channels, channels)
    chan = lax.broadcasted_iota(jnp.int32, shape, 1 if transposed else 0)
    col = lax.broadcasted_iota(jnp.int32, shape, 0 if transposed else 1)
    quarter = channels // TEAM
    mate = lax.div(col, quarter)
    within = lax.rem(col, quarter)
    slot = lax.div(within, rows)
    row = lax.rem(within, rows)
    level = jnp.zeros_like(slot)
    bit = quarter // rows // 2
    while bit:
        level = level * 2 + lax.rem(slot, 2)
        slot = lax.div(slot, 2)
        bit //= 2
    want = rows * (TEAM * (level ^ place[0]) + (mate ^ place[1])) + row
    return jnp.where(chan == want, 1.0, 0.0).astype(BF16)


def pool_kernel(rows, place, act, low, high, *mates):
    channels = act.shape[1]
    quarter = channels // TEAM
    order = relative_order(place, rows, channels, False)

    def pooled(g):
        t = g.shape[0]
        u = lax.broadcasted_iota(jnp.int32, (t // 2, t), 0)
        v = lax.broadcasted_iota(jnp.int32, (t // 2, t), 1)
        halves = jnp.where(lax.div(v, 2) == u, 0.5, 0.0).astype(BF16)
        s = jnp.dot(halves, g, preferred_element_type=F32).astype(BF16)
        return jnp.dot(s, order, preferred_element_type=F32).astype(BF16)

    def put(at, s):
        n = s.shape[0]
        for r, mate in enumerate(mates):
            mate[at : at + n, :] = s[:, r * quarter : (r + 1) * quarter]

    def gelu(v):
        return gelu_value(v.astype(F32)).astype(BF16)

    window = act.shape[0]
    block = 256
    g_prev = gelu(low[...])
    for at in range(0, window, block):
        g = gelu(act[at : at + block, :])
        joined = jnp.concatenate([g_prev, g[: block - HALO]], axis=0)
        put(at // 2, pooled(joined))
        g_prev = g[block - HALO :]
    put(window // 2, pooled(jnp.concatenate([g_prev, gelu(high[...])], axis=0)))


def team_sums(left, pairs, start):
    total = start
    for s, c in pairs:
        positions = c.shape[1]
        quarter = s.shape[1]
        for k in range(TAPS):
            at = EXT + 2 * (k - 2)
            left[k * quarter : (k + 1) * quarter, :] = s[at : at + positions, :].T
        term = lax.dot_general(
            left[...], c[...], (((1,), (1,)), ((), ())), preferred_element_type=F32
        )
        total = term if total is None else total + term
    return total


def near_kernel(s0, s1, c0, c1, out, left):
    out[...] = team_sums(left, ((s0, c0), (s1, c1)), None)


def wgrad_kernel(rows, start, s2, s3, c2, c3, *refs):
    *outs, left = refs
    quarter = s2.shape[1]
    total = team_sums(left, ((s2, c2), (s3, c3)), start[...])
    if len(outs) == 1:
        for k in range(TAPS):
            outs[0][k] = total[k * quarter : (k + 1) * quarter]
    else:
        for k in range(TAPS):
            for m, out in enumerate(outs):
                size = out.shape[1]
                at = k * quarter + m * size
                out[k] = total[at : at + size].astype(out.dtype)


def fill_ext(ext, cot, low, high):
    positions = cot.shape[0]
    ext[:HALO, :] = low[...]
    ext[HALO : HALO + positions, :] = cot[...]
    ext[HALO + positions :, :] = high[...]


def taps_of(k_a, k_b, width):
    return [jnp.concatenate([k_a[k], k_b[k]], axis=0)[:, :width] for k in range(TAPS)]


def products(columns, shifted, weights):
    acc = jnp.dot(columns, jnp.concatenate(weights, axis=0), preferred_element_type=F32)
    grad = None
    for k, weight in enumerate(weights):
        term = lax.dot_general(
            shifted[k], weight, (((1,), (1,)), ((), ())), preferred_element_type=F32
        )
        grad = term if grad is None else grad + term
    return acc, grad


def fill_columns(columns, s_a, s_b, positions):
    quarter = s_a.shape[1]
    for k in range(TAPS):
        at = EXT + 2 * (k - 2)
        for i, s in enumerate((s_a, s_b)):
            lane = (2 * k + i) * quarter
            columns[:, lane : lane + quarter] = s[at : at + positions, :]


def spread(grad, slope, doubled, back, base, out):
    positions = grad.shape[0]
    blocks, _, lanes = doubled.shape
    for j in range(blocks):
        g = grad[:, j * lanes : (j + 1) * lanes]
        doubled[j, pl.ds(0, positions, 2), :] = g
        doubled[j, pl.ds(1, positions, 2), :] = g
    block = 256
    for at in range(0, 2 * positions, block):
        rows = slice(at, at + block)
        mixed = jnp.concatenate(
            [
                (doubled[j, rows, :] * slope(rows, j * lanes, (j + 1) * lanes)).astype(BF16)
                for j in range(blocks)
            ],
            axis=1,
        )
        put = jnp.dot(mixed, back, preferred_element_type=F32)
        if base is not None:
            put = put + base[rows, :].astype(F32)
        out[rows, :] = put.astype(BF16)


def first_kernel(rows, place, s0, s1, s2, s3, k0, k1, cot, low, high, act, *refs):
    acc, part, slope, back, later, shifted, ext, columns, doubled = refs
    positions, width = cot.shape
    window, channels = act.shape
    half = channels // 2
    fill_ext(ext, cot, low, high)
    for k in range(TAPS):
        at = HALO - 2 * (k - 2)
        shifted[k] = ext[at : at + positions, :]
    fill_columns(columns, s0, s1, positions)
    fill_columns(later, s2, s3, positions)
    order = relative_order(place, rows, channels, True)
    back[...] = order[half:, :]
    acc[...], grad = products(columns[...], shifted, taps_of(k0, k1, width))

    def slope_of(rows, start, stop):
        v = lax.dot_general(
            act[rows, :], order[start:stop, :], (((1,), (1,)), ((), ())), preferred_element_type=F32
        )
        return 0.5 * gelu_slope(v)

    spread(grad, slope_of, doubled, order[:half, :], None, part)
    for at in range(0, window, 256):
        slope[at : at + 256, :] = slope_of(slice(at, at + 256), half, channels)


def second_kernel(k2, k3, columns, shifted, acc1, part, slope, back, pooled, out, doubled):
    acc, grad = products(columns[...], shifted, taps_of(k2, k3, shifted.shape[2]))
    pooled[...] = (acc + acc1[...]).astype(BF16).T
    spread(grad, lambda rows, i, j: slope[rows, i:j], doubled, back[...], part, out)


def after(x, *first):
    return lax.optimization_barrier((x, first))[0]


def flip(x, bit):
    n = lax.axis_size("pos")
    return lax.ppermute(x, "pos", [(i, i ^ bit) for i in range(n)])


def on_device(activations, kernel, cotangent):
    window, channels = activations.shape
    positions, width = cotangent.shape
    rows = kernel.shape[0]
    n = lax.axis_size("pos")
    levels = n // TEAM
    quarter = channels // TEAM
    me = lax.axis_index("pos")
    place = jnp.stack([me // TEAM, me % TEAM]).astype(jnp.int32)

    cot_t = cotangent.T
    shard = kernel.transpose(1, 0, 2)

    cot_y = flip(cot_t, 2)
    order = [0]
    blocks = [shard]
    while len(order) < levels:
        bit = levels // 2 // len(order)
        blocks = blocks + [flip(block, TEAM * bit) for block in blocks]
        order += [m ^ bit for m in order]
    k0 = jnp.concatenate(blocks, axis=1)
    early = blocks[1:2] + blocks[levels // 2 : levels // 2 + 1]
    edge_low = jnp.concatenate([activations[-HALO:], cotangent[-HALO:]], axis=1)
    edge_high = jnp.concatenate([activations[:HALO], cotangent[:HALO]], axis=1)
    low = lax.ppermute(edge_low, "pos", [(i, i + 1) for i in range(n - 1)])
    high = lax.ppermute(edge_high, "pos", [(i + 1, i) for i in range(n - 1)])
    cot_c = flip(cot_t, 1)

    ext_rows = positions + 2 * EXT
    pieces = pl.pallas_call(
        functools.partial(pool_kernel, rows),
        out_shape=[jax.ShapeDtypeStruct((ext_rows, quarter), BF16)] * TEAM,
        in_specs=[SMEM, VMEM, VMEM, VMEM],
        out_specs=[VMEM] * TEAM,
        compiler_params=params(32),
        name="pool",
    )(place, after(activations, *early), low[:, :channels], high[:, :channels])

    far = after(pieces[2:], cot_y)
    mates = [pieces[0], flip(pieces[1], 1), flip(far[0], 2), flip(far[1], 3)]
    cot_y = after(cot_y, pieces, blocks[-1])
    cot_yc = flip(cot_y, 1)

    split = rows % 16 == 0
    if split:
        grad_shape = [
            jax.ShapeDtypeStruct((TAPS, rows, width), BF16 if m else F32) for m in range(levels)
        ]
    else:
        grad_shape = [jax.ShapeDtypeStruct((TAPS, quarter, width), F32)]
    left = pltpu.VMEM((TAPS * quarter, positions), BF16)
    start = pl.pallas_call(
        near_kernel,
        out_shape=jax.ShapeDtypeStruct((TAPS * quarter, width), F32),
        in_specs=[VMEM] * 4,
        out_specs=VMEM,
        scratch_shapes=[left],
        compiler_params=params(24),
        name="near",
    )(mates[0], mates[1], cot_t, cot_c)
    grads = pl.pallas_call(
        functools.partial(wgrad_kernel, rows),
        out_shape=grad_shape,
        in_specs=[VMEM] * 5,
        out_specs=[VMEM] * len(grad_shape),
        scratch_shapes=[left],
        compiler_params=params(48),
        name="wgrad",
    )(start, mates[2], mates[3], cot_y, cot_yc)
    if not split:
        parts = [grads[0][:, m * rows : (m + 1) * rows] for m in range(levels)]
        grads = parts[:1] + [p.astype(BF16) for p in parts[1:]]
    terms = [flip(g, TEAM * m) for g, m in zip(grads[1:], order[1:])]

    k0 = after(k0, mates, cot_yc, start)
    k0 = jnp.pad(k0, ((0, 0), (0, 0), (0, -width % 128)))
    k2 = flip(k0, 2)
    k1 = flip(k0, 1)

    low_cot, high_cot = low[:, channels:], high[:, channels:]
    half = channels // 2
    doubled = pltpu.VMEM((half // 128, window, 128), F32)
    acc, part, *handed = pl.pallas_call(
        functools.partial(first_kernel, rows),
        out_shape=[
            jax.ShapeDtypeStruct((positions, width), F32),
            jax.ShapeDtypeStruct((window, channels), BF16),
            jax.ShapeDtypeStruct((window, half), F32),
            jax.ShapeDtypeStruct((half, channels), BF16),
            jax.ShapeDtypeStruct((positions, TAPS * half), BF16),
            jax.ShapeDtypeStruct((TAPS, positions, width), BF16),
        ],
        in_specs=[SMEM] + [VMEM] * 10,
        out_specs=[VMEM] * 6,
        scratch_shapes=[
            pltpu.VMEM((positions + 2 * HALO, width), BF16),
            pltpu.VMEM((positions, TAPS * half), BF16),
            doubled,
        ],
        compiler_params=params(40),
        name="first",
    )(place, *pieces, k0, k1, cotangent, low_cot, high_cot, activations)
    slope, back, columns, shifted = handed
    k2 = after(k2, acc, terms)
    k3 = flip(k2, 1)
    pooled_t, input_grad = pl.pallas_call(
        second_kernel,
        out_shape=[
            jax.ShapeDtypeStruct((width, positions), BF16),
            jax.ShapeDtypeStruct((window, channels), BF16),
        ],
        in_specs=[VMEM] * 8,
        out_specs=[VMEM] * 2,
        scratch_shapes=[doubled],
        compiler_params=params(40),
        name="second",
    )(k2, k3, columns, shifted, acc, part, slope, back)
    total = grads[0]
    for term in terms:
        total = total + term.astype(F32)
    return pooled_t.T, input_grad, total.transpose(1, 0, 2)


def solution(mesh):
    placed = (P(("groups", "pos"), None), P("pos", None, None), P(("groups", "pos"), None))
    return jax.shard_map(
        on_device,
        mesh=mesh,
        in_specs=placed,
        out_specs=(
            P(("groups", "pos"), None),
            P(("groups", "pos"), None),
            P(("groups", "pos"), None, None),
        ),
        check_vma=False,
    )
```

```python
import functools

import jax
import jax.numpy as jnp
from jax import lax
from jax.experimental import pallas as pl
from jax.experimental.pallas import tpu as pltpu
from jax.sharding import PartitionSpec as P

STEP = 4
TAPS = 5
HALO = 16
TEAM = 4
EXT = 8
VMEM = pl.BlockSpec(memory_space=pltpu.VMEM)
SMEM = pl.BlockSpec(memory_space=pltpu.SMEM)
F32 = jnp.float32
BF16 = jnp.bfloat16


def params(mib):
    return pltpu.CompilerParams(vmem_limit_bytes=mib * 2**20)


def gelu_value(v):
    return 0.5 * v * (1.0 + lax.erf(v * 0.7071067811865476))


def gelu_slope(v):
    return (
        0.5 * (1.0 + lax.erf(v * 0.7071067811865476))
        + v * jnp.exp(-0.5 * v * v) * 0.3989422804014327
    )


def relative_order(place, rows, channels, transposed):
    shape = (channels, channels)
    chan = lax.broadcasted_iota(jnp.int32, shape, 1 if transposed else 0)
    col = lax.broadcasted_iota(jnp.int32, shape, 0 if transposed else 1)
    quarter = channels // TEAM
    mate = lax.div(col, quarter)
    within = lax.rem(col, quarter)
    slot = lax.div(within, rows)
    row = lax.rem(within, rows)
    level = jnp.zeros_like(slot)
    bit = quarter // rows // 2
    while bit:
        level = level * 2 + lax.rem(slot, 2)
        slot = lax.div(slot, 2)
        bit //= 2
    want = rows * (TEAM * (level ^ place[0]) + (mate ^ place[1])) + row
    return jnp.where(chan == want, 1.0, 0.0).astype(BF16)


def pooled_gelu(v, order):
    g = gelu_value(v.astype(F32)).astype(BF16)
    t = g.shape[0]
    u = lax.broadcasted_iota(jnp.int32, (t // 2, t), 0)
    w = lax.broadcasted_iota(jnp.int32, (t // 2, t), 1)
    halves = jnp.where(lax.div(w, 2) == u, 0.5, 0.0).astype(BF16)
    s = jnp.dot(halves, g, preferred_element_type=F32).astype(BF16)
    return jnp.dot(s, order, preferred_element_type=F32).astype(BF16)


def put_quarters(outs, at, s):
    quarter = s.shape[1] // TEAM
    for r, out in enumerate(outs):
        out[at : at + s.shape[0], :] = s[:, r * quarter : (r + 1) * quarter]


def body_kernel(rows, place, act, order, *bodies):
    order[...] = relative_order(place, rows, act.shape[1], False)
    block = 256
    for at in range(0, act.shape[0], block):
        put_quarters(bodies, at // 2, pooled_gelu(act[at : at + block, :], order[...]))


def pool_kernel(order, low, high, *refs):
    bodies, outs = refs[:TEAM], refs[TEAM:]
    n = bodies[0].shape[0]
    put_quarters(outs, 0, pooled_gelu(low[...], order[...]))
    for body, out in zip(bodies, outs):
        out[EXT : EXT + n, :] = body[...]
    put_quarters(outs, EXT + n, pooled_gelu(high[...], order[...]))


def team_sums(left, pairs, start):
    total = start
    for s, c in pairs:
        positions = c.shape[1]
        quarter = s.shape[1]
        for k in range(TAPS):
            at = EXT + 2 * (k - 2)
            left[k * quarter : (k + 1) * quarter, :] = s[at : at + positions, :].T
        term = lax.dot_general(
            left[...], c[...], (((1,), (1,)), ((), ())), preferred_element_type=F32
        )
        total = term if total is None else total + term
    return total


def near_kernel(s0, s1, c0, c1, out, left):
    out[...] = team_sums(left, ((s0, c0), (s1, c1)), None)


def wgrad_kernel(rows, start, s2, s3, c2, c3, *refs):
    *outs, left = refs
    quarter = s2.shape[1]
    total = team_sums(left, ((s2, c2), (s3, c3)), start[...])
    if len(outs) == 1:
        for k in range(TAPS):
            outs[0][k] = total[k * quarter : (k + 1) * quarter]
    else:
        for k in range(TAPS):
            for m, out in enumerate(outs):
                size = out.shape[1]
                at = k * quarter + m * size
                out[k] = total[at : at + size].astype(out.dtype)


def fill_ext(ext, cot, low, high):
    positions = cot.shape[0]
    ext[:HALO, :] = low[...]
    ext[HALO : HALO + positions, :] = cot[...]
    ext[HALO + positions :, :] = high[...]


def taps_of(k_a, k_b, width):
    return [jnp.concatenate([k_a[k], k_b[k]], axis=0)[:, :width] for k in range(TAPS)]


def products(columns, shifted, weights):
    acc = jnp.dot(columns, jnp.concatenate(weights, axis=0), preferred_element_type=F32)
    grad = None
    for k, weight in enumerate(weights):
        term = lax.dot_general(
            shifted[k], weight, (((1,), (1,)), ((), ())), preferred_element_type=F32
        )
        grad = term if grad is None else grad + term
    return acc, grad


def fill_columns(columns, s_a, s_b, positions):
    quarter = s_a.shape[1]
    for k in range(TAPS):
        at = EXT + 2 * (k - 2)
        for i, s in enumerate((s_a, s_b)):
            lane = (2 * k + i) * quarter
            columns[:, lane : lane + quarter] = s[at : at + positions, :]


def spread(grad, slope, doubled, back, base, out):
    positions = grad.shape[0]
    blocks, _, lanes = doubled.shape
    for j in range(blocks):
        g = grad[:, j * lanes : (j + 1) * lanes]
        doubled[j, pl.ds(0, positions, 2), :] = g
        doubled[j, pl.ds(1, positions, 2), :] = g
    block = 256
    for at in range(0, 2 * positions, block):
        rows = slice(at, at + block)
        mixed = jnp.concatenate(
            [
                (doubled[j, rows, :] * slope(rows, j * lanes, (j + 1) * lanes)).astype(BF16)
                for j in range(blocks)
            ],
            axis=1,
        )
        put = jnp.dot(mixed, back, preferred_element_type=F32)
        if base is not None:
            put = put + base[rows, :].astype(F32)
        out[rows, :] = put.astype(BF16)


def first_kernel(rows, place, s0, s1, s2, s3, k0, k1, cot, low, high, act, *refs):
    acc, part, slope, back, later, shifted, ext, columns, doubled = refs
    positions, width = cot.shape
    window, channels = act.shape
    half = channels // 2
    fill_ext(ext, cot, low, high)
    for k in range(TAPS):
        at = HALO - 2 * (k - 2)
        shifted[k] = ext[at : at + positions, :]
    fill_columns(columns, s0, s1, positions)
    fill_columns(later, s2, s3, positions)
    order = relative_order(place, rows, channels, True)
    back[...] = order[half:, :]
    acc[...], grad = products(columns[...], shifted, taps_of(k0, k1, width))

    def slope_of(rows, start, stop):
        v = lax.dot_general(
            act[rows, :], order[start:stop, :], (((1,), (1,)), ((), ())), preferred_element_type=F32
        )
        return 0.5 * gelu_slope(v)

    spread(grad, slope_of, doubled, order[:half, :], None, part)
    for at in range(0, window, 256):
        slope[at : at + 256, :] = slope_of(slice(at, at + 256), half, channels)


def second_kernel(k2, k3, columns, shifted, acc1, part, slope, back, pooled, out, doubled):
    acc, grad = products(columns[...], shifted, taps_of(k2, k3, shifted.shape[2]))
    pooled[...] = (acc + acc1[...]).astype(BF16).T
    spread(grad, lambda rows, i, j: slope[rows, i:j], doubled, back[...], part, out)


def after(x, *first):
    return lax.optimization_barrier((x, first))[0]


def flip(x, bit):
    n = lax.axis_size("pos")
    return lax.ppermute(x, "pos", [(i, i ^ bit) for i in range(n)])


def on_device(activations, kernel, cotangent):
    window, channels = activations.shape
    positions, width = cotangent.shape
    rows = kernel.shape[0]
    n = lax.axis_size("pos")
    levels = n // TEAM
    quarter = channels // TEAM
    me = lax.axis_index("pos")
    place = jnp.stack([me // TEAM, me % TEAM]).astype(jnp.int32)

    cot_t = cotangent.T
    shard = kernel.transpose(1, 0, 2)

    cot_y = flip(cot_t, 2)
    gelu_order, *bodies = pl.pallas_call(
        functools.partial(body_kernel, rows),
        out_shape=[jax.ShapeDtypeStruct((channels, channels), BF16)]
        + [jax.ShapeDtypeStruct((positions, quarter), BF16)] * TEAM,
        in_specs=[SMEM, VMEM],
        out_specs=[VMEM] * (TEAM + 1),
        compiler_params=params(24),
        name="body",
    )(place, activations)
    order = [0]
    blocks = [shard]
    while len(order) < levels:
        bit = levels // 2 // len(order)
        received = after(blocks[1:], bodies)
        blocks = blocks + [flip(block, TEAM * bit) for block in blocks[:1] + received]
        order += [m ^ bit for m in order]
    k0 = jnp.concatenate(blocks, axis=1)
    early = blocks[1:2] + blocks[levels // 2 : levels // 2 + 1]
    edge_low = jnp.concatenate([activations[-HALO:], cotangent[-HALO:]], axis=1)
    edge_high = jnp.concatenate([activations[:HALO], cotangent[:HALO]], axis=1)
    low = lax.ppermute(edge_low, "pos", [(i, i + 1) for i in range(n - 1)])
    high = lax.ppermute(edge_high, "pos", [(i + 1, i) for i in range(n - 1)])
    cot_c = flip(cot_t, 1)

    ext_rows = positions + 2 * EXT
    pieces = pl.pallas_call(
        pool_kernel,
        out_shape=[jax.ShapeDtypeStruct((ext_rows, quarter), BF16)] * TEAM,
        in_specs=[VMEM] * (TEAM + 3),
        out_specs=[VMEM] * TEAM,
        compiler_params=params(24),
        name="pool",
    )(after(gelu_order, *early), low[:, :channels], high[:, :channels], *bodies)

    far = after(pieces[2:], cot_y)
    mates = [pieces[0], flip(pieces[1], 1), flip(far[0], 2), flip(far[1], 3)]
    cot_y = after(cot_y, pieces, blocks[-1])
    cot_yc = flip(cot_y, 1)

    split = rows % 16 == 0
    if split:
        grad_shape = [
            jax.ShapeDtypeStruct((TAPS, rows, width), BF16 if m else F32) for m in range(levels)
        ]
    else:
        grad_shape = [jax.ShapeDtypeStruct((TAPS, quarter, width), F32)]
    left = pltpu.VMEM((TAPS * quarter, positions), BF16)
    start = pl.pallas_call(
        near_kernel,
        out_shape=jax.ShapeDtypeStruct((TAPS * quarter, width), F32),
        in_specs=[VMEM] * 4,
        out_specs=VMEM,
        scratch_shapes=[left],
        compiler_params=params(24),
        name="near",
    )(mates[0], mates[1], cot_t, cot_c)
    grads = pl.pallas_call(
        functools.partial(wgrad_kernel, rows),
        out_shape=grad_shape,
        in_specs=[VMEM] * 5,
        out_specs=[VMEM] * len(grad_shape),
        scratch_shapes=[left],
        compiler_params=params(48),
        name="wgrad",
    )(start, mates[2], mates[3], cot_y, cot_yc)
    if not split:
        parts = [grads[0][:, m * rows : (m + 1) * rows] for m in range(levels)]
        grads = parts[:1] + [p.astype(BF16) for p in parts[1:]]
    terms = [flip(g, TEAM * m) for g, m in zip(grads[1:], order[1:])]

    k0 = after(k0, mates, cot_yc, start)
    k0 = jnp.pad(k0, ((0, 0), (0, 0), (0, -width % 128)))
    k2 = flip(k0, 2)
    k1 = flip(k0, 1)

    low_cot, high_cot = low[:, channels:], high[:, channels:]
    half = channels // 2
    doubled = pltpu.VMEM((half // 128, window, 128), F32)
    acc, part, *handed = pl.pallas_call(
        functools.partial(first_kernel, rows),
        out_shape=[
            jax.ShapeDtypeStruct((positions, width), F32),
            jax.ShapeDtypeStruct((window, channels), BF16),
            jax.ShapeDtypeStruct((window, half), F32),
            jax.ShapeDtypeStruct((half, channels), BF16),
            jax.ShapeDtypeStruct((positions, TAPS * half), BF16),
            jax.ShapeDtypeStruct((TAPS, positions, width), BF16),
        ],
        in_specs=[SMEM] + [VMEM] * 10,
        out_specs=[VMEM] * 6,
        scratch_shapes=[
            pltpu.VMEM((positions + 2 * HALO, width), BF16),
            pltpu.VMEM((positions, TAPS * half), BF16),
            doubled,
        ],
        compiler_params=params(40),
        name="first",
    )(place, *pieces, k0, k1, cotangent, low_cot, high_cot, activations)
    slope, back, columns, shifted = handed
    k2 = after(k2, acc, terms)
    k3 = flip(k2, 1)
    pooled_t, input_grad = pl.pallas_call(
        second_kernel,
        out_shape=[
            jax.ShapeDtypeStruct((width, positions), BF16),
            jax.ShapeDtypeStruct((window, channels), BF16),
        ],
        in_specs=[VMEM] * 8,
        out_specs=[VMEM] * 2,
        scratch_shapes=[doubled],
        compiler_params=params(40),
        name="second",
    )(k2, k3, columns, shifted, acc, part, slope, back)
    total = grads[0]
    for term in terms:
        total = total + term.astype(F32)
    return pooled_t.T, input_grad, total.transpose(1, 0, 2)


def solution(mesh):
    placed = (P(("groups", "pos"), None), P("pos", None, None), P(("groups", "pos"), None))
    return jax.shard_map(
        on_device,
        mesh=mesh,
        in_specs=placed,
        out_specs=(
            P(("groups", "pos"), None),
            P(("groups", "pos"), None),
            P(("groups", "pos"), None, None),
        ),
        check_vma=False,
    )
```

```python
import functools

import jax
import jax.numpy as jnp
from jax import lax
from jax.experimental import pallas as pl
from jax.experimental.pallas import tpu as pltpu
from jax.sharding import PartitionSpec as P

STEP = 4
TAPS = 5
HALO = 16
TEAM = 4
EXT = 8
VMEM = pl.BlockSpec(memory_space=pltpu.VMEM)
SMEM = pl.BlockSpec(memory_space=pltpu.SMEM)
F32 = jnp.float32
BF16 = jnp.bfloat16


def params(mib):
    return pltpu.CompilerParams(vmem_limit_bytes=mib * 2**20)


def gelu_value(v):
    return 0.5 * v * (1.0 + lax.erf(v * 0.7071067811865476))


def gelu_slope(v):
    return (
        0.5 * (1.0 + lax.erf(v * 0.7071067811865476))
        + v * jnp.exp(-0.5 * v * v) * 0.3989422804014327
    )


def relative_order(place, rows, channels, transposed):
    shape = (channels, channels)
    chan = lax.broadcasted_iota(jnp.int32, shape, 1 if transposed else 0)
    col = lax.broadcasted_iota(jnp.int32, shape, 0 if transposed else 1)
    quarter = channels // TEAM
    mate = lax.div(col, quarter)
    within = lax.rem(col, quarter)
    slot = lax.div(within, rows)
    row = lax.rem(within, rows)
    level = jnp.zeros_like(slot)
    bit = quarter // rows // 2
    while bit:
        level = level * 2 + lax.rem(slot, 2)
        slot = lax.div(slot, 2)
        bit //= 2
    want = rows * (TEAM * (level ^ place[0]) + (mate ^ place[1])) + row
    return jnp.where(chan == want, 1.0, 0.0).astype(BF16)


def pooled_gelu(v, order):
    g = gelu_value(v.astype(F32)).astype(BF16)
    t = g.shape[0]
    u = lax.broadcasted_iota(jnp.int32, (t // 2, t), 0)
    w = lax.broadcasted_iota(jnp.int32, (t // 2, t), 1)
    halves = jnp.where(lax.div(w, 2) == u, 0.5, 0.0).astype(BF16)
    s = jnp.dot(halves, g, preferred_element_type=F32).astype(BF16)
    return jnp.dot(s, order, preferred_element_type=F32).astype(BF16)


def put_quarters(outs, at, s):
    quarter = s.shape[1] // TEAM
    for r, out in enumerate(outs):
        out[at : at + s.shape[0], :] = s[:, r * quarter : (r + 1) * quarter]


def body_kernel(rows, place, act, order, *bodies):
    order[...] = relative_order(place, rows, act.shape[1], False)
    block = 256
    for at in range(0, act.shape[0], block):
        put_quarters(bodies, at // 2, pooled_gelu(act[at : at + block, :], order[...]))


def pool_kernel(order, low, high, *refs):
    bodies, outs = refs[:TEAM], refs[TEAM:]
    n = bodies[0].shape[0]
    put_quarters(outs, 0, pooled_gelu(low[...], order[...]))
    for body, out in zip(bodies, outs):
        out[EXT : EXT + n, :] = body[...]
    put_quarters(outs, EXT + n, pooled_gelu(high[...], order[...]))


def team_sums(left, pairs, start):
    total = start
    for s, c in pairs:
        positions = c.shape[1]
        quarter = s.shape[1]
        for k in range(TAPS):
            at = EXT + 2 * (k - 2)
            left[k * quarter : (k + 1) * quarter, :] = s[at : at + positions, :].T
        term = lax.dot_general(
            left[...], c[...], (((1,), (1,)), ((), ())), preferred_element_type=F32
        )
        total = term if total is None else total + term
    return total


def near_kernel(s0, s1, c0, c1, out, left):
    out[...] = team_sums(left, ((s0, c0), (s1, c1)), None)


def wgrad_kernel(rows, start, s2, s3, c2, c3, *refs):
    *outs, left = refs
    quarter = s2.shape[1]
    total = team_sums(left, ((s2, c2), (s3, c3)), start[...])
    if len(outs) == 1:
        for k in range(TAPS):
            outs[0][k] = total[k * quarter : (k + 1) * quarter]
    else:
        for k in range(TAPS):
            for m, out in enumerate(outs):
                size = out.shape[1]
                at = k * quarter + m * size
                out[k] = total[at : at + size].astype(out.dtype)


def fill_ext(ext, cot, low, high):
    positions = cot.shape[0]
    ext[:HALO, :] = low[...]
    ext[HALO : HALO + positions, :] = cot[...]
    ext[HALO + positions :, :] = high[...]


def taps_of(k_a, k_b, width):
    return [jnp.concatenate([k_a[k], k_b[k]], axis=0)[:, :width] for k in range(TAPS)]


def products(columns, shifted, weights):
    acc = jnp.dot(columns, jnp.concatenate(weights, axis=0), preferred_element_type=F32)
    grad = None
    for k, weight in enumerate(weights):
        term = lax.dot_general(
            shifted[k], weight, (((1,), (1,)), ((), ())), preferred_element_type=F32
        )
        grad = term if grad is None else grad + term
    return acc, grad


def fill_columns(columns, s_a, s_b, positions):
    quarter = s_a.shape[1]
    for k in range(TAPS):
        at = EXT + 2 * (k - 2)
        for i, s in enumerate((s_a, s_b)):
            lane = (2 * k + i) * quarter
            columns[:, lane : lane + quarter] = s[at : at + positions, :]


def spread(grad, slope, doubled, back, base, out):
    positions = grad.shape[0]
    blocks, _, lanes = doubled.shape
    for j in range(blocks):
        g = grad[:, j * lanes : (j + 1) * lanes]
        doubled[j, pl.ds(0, positions, 2), :] = g
        doubled[j, pl.ds(1, positions, 2), :] = g
    block = 256
    for at in range(0, 2 * positions, block):
        rows = slice(at, at + block)
        mixed = jnp.concatenate(
            [
                (doubled[j, rows, :] * slope(rows, j * lanes, (j + 1) * lanes)).astype(BF16)
                for j in range(blocks)
            ],
            axis=1,
        )
        put = jnp.dot(mixed, back, preferred_element_type=F32)
        if base is not None:
            put = put + base[rows, :].astype(F32)
        out[rows, :] = put.astype(BF16)


def first_kernel(rows, place, s0, s1, s2, s3, k0, k1, cot, low, high, act, *refs):
    acc, part, slope, back, later, shifted, ext, columns, doubled = refs
    positions, width = cot.shape
    window, channels = act.shape
    half = channels // 2
    fill_ext(ext, cot, low, high)
    for k in range(TAPS):
        at = HALO - 2 * (k - 2)
        shifted[k] = ext[at : at + positions, :]
    fill_columns(columns, s0, s1, positions)
    fill_columns(later, s2, s3, positions)
    order = relative_order(place, rows, channels, True)
    back[...] = order[half:, :]
    acc[...], grad = products(columns[...], shifted, taps_of(k0, k1, width))

    def slope_of(rows, start, stop):
        v = lax.dot_general(
            act[rows, :], order[start:stop, :], (((1,), (1,)), ((), ())), preferred_element_type=F32
        )
        return 0.5 * gelu_slope(v)

    spread(grad, slope_of, doubled, order[:half, :], None, part)
    for at in range(0, window, 256):
        slope[at : at + 256, :] = slope_of(slice(at, at + 256), half, channels)


def second_kernel(k2, k3, columns, shifted, acc1, part, slope, back, pooled, out, doubled):
    acc, grad = products(columns[...], shifted, taps_of(k2, k3, shifted.shape[2]))
    pooled[...] = (acc + acc1[...]).astype(BF16).T
    spread(grad, lambda rows, i, j: slope[rows, i:j], doubled, back[...], part, out)


def after(x, *first):
    return lax.optimization_barrier((x, first))[0]


def flip(x, bit):
    n = lax.axis_size("pos")
    return lax.ppermute(x, "pos", [(i, i ^ bit) for i in range(n)])


def on_device(activations, kernel, cotangent):
    window, channels = activations.shape
    positions, width = cotangent.shape
    rows = kernel.shape[0]
    n = lax.axis_size("pos")
    levels = n // TEAM
    quarter = channels // TEAM
    me = lax.axis_index("pos")
    place = jnp.stack([me // TEAM, me % TEAM]).astype(jnp.int32)

    cot_t = cotangent.T
    shard = kernel.transpose(1, 0, 2)

    cot_y = flip(cot_t, 2)
    gelu_order, *bodies = pl.pallas_call(
        functools.partial(body_kernel, rows),
        out_shape=[jax.ShapeDtypeStruct((channels, channels), BF16)]
        + [jax.ShapeDtypeStruct((positions, quarter), BF16)] * TEAM,
        in_specs=[SMEM, VMEM],
        out_specs=[VMEM] * (TEAM + 1),
        compiler_params=params(24),
        name="body",
    )(place, activations)
    order = [0]
    blocks = [shard]
    while len(order) < levels:
        bit = levels // 2 // len(order)
        received = after(blocks[1:], bodies)
        blocks = blocks + [flip(block, TEAM * bit) for block in blocks[:1] + received]
        order += [m ^ bit for m in order]
    k0 = jnp.concatenate(blocks, axis=1)
    early = blocks[1:2] + blocks[levels // 2 : levels // 2 + 1]
    edge_low = jnp.concatenate([activations[-HALO:], cotangent[-HALO:]], axis=1)
    edge_high = jnp.concatenate([activations[:HALO], cotangent[:HALO]], axis=1)
    low = lax.ppermute(edge_low, "pos", [(i, i + 1) for i in range(n - 1)])
    high = lax.ppermute(edge_high, "pos", [(i + 1, i) for i in range(n - 1)])
    cot_c = flip(cot_t, 1)

    ext_rows = positions + 2 * EXT
    pieces = pl.pallas_call(
        pool_kernel,
        out_shape=[jax.ShapeDtypeStruct((ext_rows, quarter), BF16)] * TEAM,
        in_specs=[VMEM] * (TEAM + 3),
        out_specs=[VMEM] * TEAM,
        compiler_params=params(24),
        name="pool",
    )(after(gelu_order, *early), low[:, :channels], high[:, :channels], *bodies)

    far = after(pieces[2:], cot_y)
    mates = [pieces[0], flip(pieces[1], 1), flip(far[0], 2), flip(far[1], 3)]
    cot_y = after(cot_y, pieces, blocks[-1])
    cot_yc = flip(cot_y, 1)

    split = rows % 16 == 0
    if split:
        grad_shape = [
            jax.ShapeDtypeStruct((TAPS, rows, width), BF16 if m else F32) for m in range(levels)
        ]
    else:
        grad_shape = [jax.ShapeDtypeStruct((TAPS, quarter, width), F32)]
    left = pltpu.VMEM((TAPS * quarter, positions), BF16)
    start = pl.pallas_call(
        near_kernel,
        out_shape=jax.ShapeDtypeStruct((TAPS * quarter, width), F32),
        in_specs=[VMEM] * 4,
        out_specs=VMEM,
        scratch_shapes=[left],
        compiler_params=params(24),
        name="near",
    )(mates[0], mates[1], cot_t, cot_c)
    grads = pl.pallas_call(
        functools.partial(wgrad_kernel, rows),
        out_shape=grad_shape,
        in_specs=[VMEM] * 5,
        out_specs=[VMEM] * len(grad_shape),
        scratch_shapes=[left],
        compiler_params=params(48),
        name="wgrad",
    )(start, mates[2], mates[3], cot_y, cot_yc)
    if not split:
        parts = [grads[0][:, m * rows : (m + 1) * rows] for m in range(levels)]
        grads = parts[:1] + [p.astype(BF16) for p in parts[1:]]
    terms = [flip(g, TEAM * m) for g, m in zip(grads[1:], order[1:])]

    k0 = jnp.pad(k0, ((0, 0), (0, 0), (0, -width % 128)))
    k0 = after(k0, start)
    k1 = flip(k0, 1)
    k2 = flip(after(k0, mates, cot_yc), 2)

    low_cot, high_cot = low[:, channels:], high[:, channels:]
    half = channels // 2
    doubled = pltpu.VMEM((half // 128, window, 128), F32)
    acc, part, *handed = pl.pallas_call(
        functools.partial(first_kernel, rows),
        out_shape=[
            jax.ShapeDtypeStruct((positions, width), F32),
            jax.ShapeDtypeStruct((window, channels), BF16),
            jax.ShapeDtypeStruct((window, half), F32),
            jax.ShapeDtypeStruct((half, channels), BF16),
            jax.ShapeDtypeStruct((positions, TAPS * half), BF16),
            jax.ShapeDtypeStruct((TAPS, positions, width), BF16),
        ],
        in_specs=[SMEM] + [VMEM] * 10,
        out_specs=[VMEM] * 6,
        scratch_shapes=[
            pltpu.VMEM((positions + 2 * HALO, width), BF16),
            pltpu.VMEM((positions, TAPS * half), BF16),
            doubled,
        ],
        compiler_params=params(40),
        name="first",
    )(place, *pieces, k0, k1, cotangent, low_cot, high_cot, activations)
    slope, back, columns, shifted = handed
    k2 = after(k2, acc, terms)
    k3 = flip(k2, 1)
    pooled_t, input_grad = pl.pallas_call(
        second_kernel,
        out_shape=[
            jax.ShapeDtypeStruct((width, positions), BF16),
            jax.ShapeDtypeStruct((window, channels), BF16),
        ],
        in_specs=[VMEM] * 8,
        out_specs=[VMEM] * 2,
        scratch_shapes=[doubled],
        compiler_params=params(40),
        name="second",
    )(k2, k3, columns, shifted, acc, part, slope, back)
    total = grads[0]
    for term in terms:
        total = total + term.astype(F32)
    return pooled_t.T, input_grad, total.transpose(1, 0, 2)


def solution(mesh):
    placed = (P(("groups", "pos"), None), P("pos", None, None), P(("groups", "pos"), None))
    return jax.shard_map(
        on_device,
        mesh=mesh,
        in_specs=placed,
        out_specs=(
            P(("groups", "pos"), None),
            P(("groups", "pos"), None),
            P(("groups", "pos"), None, None),
        ),
        check_vma=False,
    )
```
